32 devices in a mesh: cuts: 4 (over y, core), stem: 8 (over z, x).
Axes of the slice: x: 2, y: 2, z: 4, core: 2. Of those that a mesh axis runs over, the one named last changes fastest.
Arguments:
- stem_tensor: float32 [2048, 1024], P(('cuts', 'stem')), parts along dimension 0, may hold values from -0.25 to 0.25
- stem_cotangent: float32 [2048, 1024], P(('cuts', 'stem')), parts along dimension 0, may hold values from -6 to 6
- branch_tensor: bfloat16 [1024, 1024], P('stem'), may hold values from -0.1875 to 0.1875
- bit_order: int32 [16], replicated, may hold values from 0 to 15, each once
Outputs:
- stem_grad: float32 [2048, 1024], P(('cuts', 'stem')), parts along dimension 0
- branch_grad: float32 [4096, 1024], P(('cuts', 'stem')), parts along dimension 0
The draws below stay inside these ranges and needn't reach their ends.
There are 4 independent parts, one for each index of `cuts`. The reference program is written for one: setup_inputs(seed, part) draws one part's arguments, and reference() takes and returns one part's arrays. A program takes and returns all parts, laid end to end along the dimension named above; an argument that names none is the same for every part. Nothing has to cross between parts.
Inputs may be any that keep to these rules, and one draw needn't show every extreme that they name: `bit_order`: a permutation of the 16 local index bit positions.
All inputs are finite; a program needn't handle non-finite values.
Results may differ from the reference program's by a relative error of at most 0.0003.
Values may be sent and summed in bfloat16 or wider, within the bound.
A program may use at most 64 MiB of HBM per device.

```python
import jax
import jax.numpy as jnp
from jax import lax

BRANCH = 1024
ROWS_DEV = 64
STEM_ROWS = 512
DEV_BITS = 3
LOCAL_BITS = 16
N_STEM = 8


def level_of(rng, shape, split, smallest, high):
    def one(axis_at, shards_of):
        draws = jax.random.uniform(jax.random.fold_in(jax.random.fold_in(rng, 6), axis_at), (shards_of,), jnp.float32, smallest / len(split), high / len(split))
        return jnp.repeat(jnp.exp(draws), shape[axis_at] // shards_of).reshape((-1,) + (1,) * (len(shape) - axis_at - 1))

    level = one(*split[0])
    for cut in split[1:]:
        level = level * one(*cut)
    return level


def normal_values(stream_key, dims, width, limit, shards=(), held_as=jnp.bfloat16):
    values = jax.random.normal(stream_key, dims, jnp.float32) * width
    if len(shards) > 0:
        values = level_of(stream_key, dims, shards, -0.22, 0.18) * values
    return jnp.clip(values, min=-limit, max=limit).astype(held_as)


def setup_inputs(seed: int = 0, part: int = 0) -> dict:
    seeds = jax.random.split(jax.random.key(seed), 5)
    part_splits = jax.random.split(jax.random.fold_in(seeds[4], part), 5)
    stem_tensor = normal_values(part_splits[0], (STEM_ROWS, BRANCH), STEM_ROWS ** -0.5, 0.25, ((0, 8),), jnp.float32)
    stem_cotangent = normal_values(part_splits[1], (STEM_ROWS, BRANCH), 1.0, 6.0, ((0, 8),), jnp.float32)
    branch_tensor = normal_values(seeds[2], (BRANCH, BRANCH), BRANCH ** -0.5, 0.1875, ((0, 8),))
    bit_order = jax.random.permutation(seeds[3], LOCAL_BITS).astype(jnp.int32)
    return {"stem_tensor": stem_tensor, "stem_cotangent": stem_cotangent, "branch_tensor": branch_tensor, "bit_order": bit_order}


def bit_tables(bit_order, local_bits, dev_bits):
    local_size = 2 ** local_bits
    positions = jnp.arange(local_size, dtype=jnp.int32)
    forward = jnp.zeros((local_size,), jnp.int32)
    backward = jnp.zeros((local_size,), jnp.int32)
    for order_pos in range(local_bits):
        if order_pos < dev_bits:
            target_bit = dev_bits - 1 - order_pos
        else:
            target_bit = dev_bits + local_bits - 1 - order_pos
        source = bit_order[order_pos].astype(jnp.int32)
        forward = forward + jnp.left_shift(jnp.right_shift(positions, source) & 1, target_bit)
        backward = backward + jnp.left_shift(jnp.right_shift(positions, target_bit) & 1, source)
    return forward, backward


def reference(stem_tensor, stem_cotangent, branch_tensor, bit_order):
    local_size = ROWS_DEV * BRANCH
    free_size = local_size // N_STEM
    forward, backward = bit_tables(bit_order, LOCAL_BITS, DEV_BITS)
    arranged = jnp.take(stem_tensor.reshape(N_STEM, local_size), backward, axis=1)
    perm_stem = arranged.reshape(N_STEM, free_size, N_STEM).transpose(2, 1, 0).reshape(STEM_ROWS, BRANCH)
    branch_grad = jnp.dot(perm_stem.T, stem_cotangent, precision=lax.Precision.HIGHEST, preferred_element_type=jnp.float32)
    perm_adjoint = jnp.dot(stem_cotangent, branch_tensor.astype(jnp.float32).T, precision=lax.Precision.HIGHEST, preferred_element_type=jnp.float32)
    returned = perm_adjoint.reshape(N_STEM, free_size, N_STEM).transpose(2, 1, 0).reshape(N_STEM, local_size)
    stem_grad = jnp.take(returned, forward, axis=1).reshape(STEM_ROWS, BRANCH)
    return stem_grad, branch_grad
```

```python
import functools

import jax
import jax.numpy as jnp
from jax import lax
from jax.experimental import pallas as pl
from jax.experimental.pallas import tpu as pltpu
from jax.sharding import PartitionSpec as P

LANES = 128
LANE_BITS = 7


def bit_tables(bit_order, local_bits, dev_bits):
    local_size = 2**local_bits
    positions = jnp.arange(local_size, dtype=jnp.int32)
    forward = jnp.zeros((local_size,), jnp.int32)
    backward = jnp.zeros((local_size,), jnp.int32)
    for order_pos in range(local_bits):
        if order_pos < dev_bits:
            target_bit = dev_bits - 1 - order_pos
        else:
            target_bit = dev_bits + local_bits - 1 - order_pos
        source = bit_order[order_pos]
        forward = forward + jnp.left_shift(jnp.right_shift(positions, source) & 1, target_bit)
        backward = backward + jnp.left_shift(jnp.right_shift(positions, target_bit) & 1, source)
    return (forward, backward)


def per_device_wide(stem_tensor, stem_cotangent, branch_tensor, bit_order):
    members = lax.axis_size("stem")
    dev_bits = members.bit_length() - 1
    row_count, width = stem_tensor.shape
    local_size = row_count * width
    local_bits = local_size.bit_length() - 1
    free_size = local_size // members
    forward, backward = bit_tables(bit_order, local_bits, dev_bits)
    arranged = jnp.take(stem_tensor.reshape(local_size), backward).reshape(free_size, members)
    gathered = lax.all_gather(branch_tensor, "stem", axis=0, tiled=True)
    adjoint = lax.dot_general(
        stem_cotangent,
        gathered.astype(jnp.float32),
        (((1,), (1,)), ((), ())),
        precision=lax.Precision.HIGHEST,
        preferred_element_type=jnp.float32,
    )
    moved = lax.all_to_all(arranged, "stem", split_axis=1, concat_axis=1, tiled=True)
    returned = lax.all_to_all(adjoint.reshape(free_size, members), "stem", split_axis=1, concat_axis=1, tiled=True)
    perm_stem = moved.reshape(row_count, width)
    branch_term = lax.dot_general(
        perm_stem,
        stem_cotangent,
        (((0,), (0,)), ((), ())),
        precision=lax.Precision.HIGHEST,
        preferred_element_type=jnp.float32,
    )
    branch_grad = lax.psum_scatter(branch_term, "stem", scatter_dimension=0, tiled=True)
    stem_grad = jnp.take(returned.reshape(local_size), forward).reshape(row_count, width)
    return (stem_grad, branch_grad)


def split2(x):
    hi = x.astype(jnp.bfloat16)
    lo = (x - hi.astype(jnp.float32)).astype(jnp.bfloat16)
    return hi, lo


def dot(a, b):
    return jnp.dot(a, b, preferred_element_type=jnp.float32)


def dot_t(a, b):
    return lax.dot_general(a, b, (((1,), (1,)), ((), ())), preferred_element_type=jnp.float32)


def one_hot(index, rows):
    return (lax.broadcasted_iota(jnp.int32, (rows, index.shape[1]), 0) == index).astype(jnp.float32).astype(jnp.bfloat16)


def iota_row(size):
    return lax.broadcasted_iota(jnp.int32, (1, size), 1)


def permute_plan(pairs, rows):
    row_bits = rows.bit_length() - 1
    lane, row = iota_row(LANES), iota_row(rows)
    pre_lane, post_lane = jnp.zeros_like(lane), jnp.zeros_like(lane)
    pre_row, post_row = jnp.zeros_like(row), jnp.zeros_like(row)
    zero, one = jnp.int32(0), jnp.int32(1)
    moved_l, moved_r, kept_l, kept_r = zero, zero, zero, zero
    for i, o in pairs:
        i, o = jnp.int32(i), jnp.int32(o)
        li = jnp.where(i < LANE_BITS, one, zero)
        lo = jnp.where(o < LANE_BITS, one, zero)
        mid = jnp.where(
            li == 1,
            jnp.where(lo == 1, LANE_BITS - 1 - kept_l, moved_l),
            jnp.where(lo == 1, moved_r, row_bits - 1 - kept_r),
        )
        moved_l = moved_l + li * (1 - lo)
        moved_r = moved_r + (1 - li) * lo
        kept_l = kept_l + li * lo
        kept_r = kept_r + (1 - li) * (1 - lo)
        i_lane, i_row = i * li, (i - LANE_BITS) * (1 - li)
        o_lane, o_row = o * lo, (o - LANE_BITS) * (1 - lo)
        pre_lane = pre_lane + ((lane >> (mid * li)) & li) * (one << i_lane)
        pre_row = pre_row + ((row >> i_row) & (1 - li)) * (one << (mid * (1 - li)))
        post_lane = post_lane + ((lane >> o_lane) & lo) * (one << (mid * lo))
        post_row = post_row + ((row >> (mid * (1 - lo))) & (1 - lo)) * (one << o_row)
    return pre_lane, pre_row, post_lane, post_row, moved_l


def rows_times(m, x):
    hi, lo = split2(x)
    y = dot(m, jnp.concatenate([hi, lo], axis=1))
    return y[:, :LANES] + y[:, LANES:]


def lanes_times(x, m):
    hi, lo = split2(x)
    y = dot(jnp.concatenate([hi, lo], axis=0), m)
    return y[: x.shape[0]] + y[x.shape[0] :]


def permute_bits(x, plan):
    rows = x.shape[0]
    pre_lane, pre_row, post_lane, post_row, moved = plan
    x = lanes_times(x, one_hot(pre_lane, LANES))
    x = rows_times(one_hot(pre_row, rows), x)
    ri = lax.broadcasted_iota(jnp.int32, (rows, LANES), 0)
    ci = lax.broadcasted_iota(jnp.int32, (rows, LANES), 1)
    for s in range(LANE_BITS):
        step = 1 << s
        active = jnp.where(moved > s, jnp.int32(1), jnp.int32(0))
        up = pltpu.roll(pltpu.roll(x, rows - step, 0), step, 1)
        down = pltpu.roll(pltpu.roll(x, step, 0), LANES - step, 1)
        diff = (((ci >> s) & 1) - ((ri >> s) & 1)) * active
        x = jnp.where(diff == 1, up, jnp.where(diff == -1, down, x))
    x = rows_times(one_hot(post_row, rows), x)
    return lanes_times(x, one_hot(post_lane, LANES))


def kernel(n, order, stem, cot, branch, stem_grad, branch_grad, gat, bsend, brecv, ssend, srecv, gss, grs, bss, brs, sss, srs):
    me = lax.axis_index("stem")
    rows, width = stem.shape
    tiles = width // LANES
    flat_rows = rows * tiles
    part = branch.shape[0] // n
    row_bits = rows.bit_length() - 1
    tile_bits = tiles.bit_length() - 1
    dev_bits = n.bit_length() - 1
    part_bits = part.bit_length() - 1
    local_bits = row_bits + tile_bits + LANE_BITS
    high_bits = local_bits - 2 * LANE_BITS
    cols = 2
    nz = n // cols
    z, x = me // cols, me % cols
    up_dev = jnp.minimum(me + cols, n - 1)
    dn_dev = jnp.maximum(me - cols, 0)
    x_dev = z * cols + (1 - x)

    barrier = pltpu.get_barrier_semaphore()
    for off in range(1, n):
        pl.semaphore_signal(barrier, inc=1, device_id={"stem": (me + off) % n}, device_id_type=pl.DeviceIdType.MESH)

    hi, lo = split2(cot[...])
    mine = pl.ds(pl.multiple_of(me * rows, rows), rows)
    gat[0, mine, :] = hi
    gat[1, mine, :] = lo
    pl.semaphore_wait(barrier, n - 1)

    UP, DOWN, ACROSS = 0, 1, 2
    targets = (up_dev, dn_dev, x_dev)

    def block(h, o, way):
        place = gat.at[h, pl.ds(pl.multiple_of(o * rows, rows), rows)]
        return pltpu.make_async_remote_copy(
            src_ref=place,
            dst_ref=place,
            send_sem=gss.at[h, o, way],
            recv_sem=grs.at[h, o],
            device_id={"stem": targets[way]},
            device_id_type=pl.DeviceIdType.MESH,
        )

    def exists(way):
        return (z < nz - 1, z > 0, z >= 0)[way]

    def send(h, o, way):
        @pl.when(exists(way))
        def _():
            block(h, o, way).start()

    def arrive(h, o):
        block(h, o, ACROSS).wait_recv()

    def sent(h, o, way):
        @pl.when(exists(way))
        def _():
            block(h, o, way).wait_send()

    for h in (0, 1):
        for way in (UP, DOWN, ACROSS):
            send(h, me, way)

    at = iota_row(n * part)
    pick = one_hot((at % n) * part + at // n, n * part)
    bsend[...] = dot(pick, branch[...]).astype(jnp.bfloat16).reshape(n, part, width)

    def direct(src, dst, sems, rsems, off):
        peer = (me + off) % n
        return pltpu.make_async_remote_copy(
            src_ref=src.at[peer],
            dst_ref=dst.at[me],
            send_sem=sems.at[off],
            recv_sem=rsems.at[me],
            device_id={"stem": peer},
            device_id_type=pl.DeviceIdType.MESH,
        )

    def direct_in(src, dst, sems, rsems, off):
        peer = (me + off) % n
        return pltpu.make_async_remote_copy(
            src_ref=src.at[peer],
            dst_ref=dst.at[peer],
            send_sem=sems.at[off],
            recv_sem=rsems.at[peer],
            device_id={"stem": peer},
            device_id_type=pl.DeviceIdType.MESH,
        )

    for off in range(1, n):
        direct(bsend, brecv, bss, brs, off).start()
    brecv[me] = bsend[me]

    arrive(0, x_dev)
    send(0, x_dev, UP)
    send(0, x_dev, DOWN)

    def held(i):
        return jnp.where(i < LANE_BITS, i, jnp.where(i < LANE_BITS + tile_bits, i + row_bits, i - tile_bits))

    def placed(p):
        if p < part_bits:
            return LANE_BITS + p
        if p < LANE_BITS:
            return local_bits - dev_bits + p - part_bits
        if p < 2 * LANE_BITS:
            return p - LANE_BITS
        return LANE_BITS + part_bits + p - 2 * LANE_BITS

    spots = [held(order[m]) for m in range(local_bits)]
    plan = permute_plan([(spots[m], placed(local_bits - 1 - m)) for m in range(local_bits)], flat_rows)
    flat = jnp.concatenate([stem[:, t * LANES : (t + 1) * LANES] for t in range(tiles)], axis=0)
    ssend[...] = permute_bits(flat, plan).reshape(n, flat_rows // n, LANES)
    for off in range(1, n):
        direct(ssend, srecv, sss, srs, off).start()
    srecv[me] = ssend[me]

    for k in range(1, nz):
        @pl.when(z - k >= 0)
        def _():
            for xo in range(cols):
                o = (z - k) * cols + xo
                arrive(0, o)
                send(0, o, UP)
            o = (z - k) * cols + x
            arrive(1, o)
            send(1, o, UP)
            send(1, o, ACROSS)

        @pl.when(z + k <= nz - 1)
        def _():
            for xo in range(cols):
                o = (z + k) * cols + xo
                arrive(0, o)
                send(0, o, DOWN)
            o = (z + k) * cols + x
            arrive(1, o)
            send(1, o, DOWN)
            send(1, o, ACROSS)

    for zz in range(nz):
        arrive(1, zz * cols + (1 - x))
    for off in range(1, n):
        direct_in(bsend, brecv, bss, brs, off).wait_recv()

    taken = brecv[...].reshape(n * part, width)
    adjoint = dot_t(gat[0], taken) + dot_t(gat[1], taken)
    plan = permute_plan([(local_bits - 1 - m, spots[m]) for m in range(local_bits)], flat_rows)
    back = permute_bits(adjoint, plan)
    for t in range(tiles):
        stem_grad[:, t * LANES : (t + 1) * LANES] = back[t * rows : (t + 1) * rows]

    for off in range(1, n):
        direct_in(ssend, srecv, sss, srs, off).wait_recv()
    highs = 1 << high_bits
    lhs = jnp.concatenate(
        [srecv[:, e * part : (e + 1) * part, :].reshape(n * part, LANES) for e in range(highs)], axis=1
    )
    hi, lo = split2(lhs)
    at = iota_row(n * part)
    mix = one_hot((at % part) * n + at // part, n * part)
    hi = dot(mix, hi).astype(jnp.bfloat16)
    lo = dot(mix, lo).astype(jnp.bfloat16)
    branch_grad[...] = dot(hi, gat[0]) + (dot(hi, gat[1]) + dot(lo, gat[0]))

    for off in range(1, n):
        direct(bsend, brecv, bss, brs, off).wait_send()
        direct(ssend, srecv, sss, srs, off).wait_send()
    for h in (0, 1):
        for way in (UP, DOWN, ACROSS):
            sent(h, me, way)
    sent(0, x_dev, UP)
    sent(0, x_dev, DOWN)
    for k in range(1, nz):
        @pl.when(z - k >= 0)
        def _():
            for xo in range(cols):
                sent(0, (z - k) * cols + xo, UP)
            o = (z - k) * cols + x
            sent(1, o, UP)
            sent(1, o, ACROSS)

        @pl.when(z + k <= nz - 1)
        def _():
            for xo in range(cols):
                sent(0, (z + k) * cols + xo, DOWN)
            o = (z + k) * cols + x
            sent(1, o, DOWN)
            sent(1, o, ACROSS)


def per_device(stem_tensor, stem_cotangent, branch_tensor, bit_order):
    n = lax.axis_size("stem")
    rows, width = stem_tensor.shape
    flat_rows = rows * width // LANES
    if n != 8 or width != n * LANES or branch_tensor.shape[0] != LANES or (rows, flat_rows) != (64, 512):
        return per_device_wide(stem_tensor, stem_cotangent, branch_tensor, bit_order)
    part = branch_tensor.shape[0] // n
    vmem = pl.BlockSpec(memory_space=pltpu.VMEM)
    dma = pltpu.SemaphoreType.DMA
    return pl.pallas_call(
        functools.partial(kernel, n),
        out_shape=(
            jax.ShapeDtypeStruct((rows, width), jnp.float32),
            jax.ShapeDtypeStruct(branch_tensor.shape, jnp.float32),
        ),
        in_specs=[pl.BlockSpec(memory_space=pltpu.SMEM), vmem, vmem, vmem],
        out_specs=(vmem, vmem),
        scratch_shapes=[
            pltpu.VMEM((2, n * rows, width), jnp.bfloat16),
            pltpu.VMEM((n, part, width), jnp.bfloat16),
            pltpu.VMEM((n, part, width), jnp.bfloat16),
            pltpu.VMEM((n, flat_rows // n, LANES), jnp.float32),
            pltpu.VMEM((n, flat_rows // n, LANES), jnp.float32),
            dma((2, n, 3)),
            dma((2, n)),
            dma((n,)),
            dma((n,)),
            dma((n,)),
            dma((n,)),
        ],
        compiler_params=pltpu.CompilerParams(
            collective_id=0, has_side_effects=True, vmem_limit_bytes=40 * 1024 * 1024
        ),
    )(bit_order, stem_tensor, stem_cotangent, branch_tensor)


def solution(mesh):
    placed = (P(("cuts", "stem"), None), P(("cuts", "stem"), None), P("stem", None), P())
    return jax.shard_map(
        per_device,
        mesh=mesh,
        in_specs=placed,
        out_specs=(P(("cuts", "stem"), None), P(("cuts", "stem"), None)),
        check_vma=False,
    )
```

```python
import functools

import jax
import jax.numpy as jnp
from jax import lax
from jax.experimental import pallas as pl
from jax.experimental.pallas import tpu as pltpu
from jax.sharding import PartitionSpec as P

LANES = 128
LANE_BITS = 7
CODES = 32767.0
KINDS = "BB"


def bit_tables(bit_order, local_bits, dev_bits):
    local_size = 2**local_bits
    positions = jnp.arange(local_size, dtype=jnp.int32)
    forward = jnp.zeros((local_size,), jnp.int32)
    backward = jnp.zeros((local_size,), jnp.int32)
    for order_pos in range(local_bits):
        if order_pos < dev_bits:
            target_bit = dev_bits - 1 - order_pos
        else:
            target_bit = dev_bits + local_bits - 1 - order_pos
        source = bit_order[order_pos]
        forward = forward + jnp.left_shift(jnp.right_shift(positions, source) & 1, target_bit)
        backward = backward + jnp.left_shift(jnp.right_shift(positions, target_bit) & 1, source)
    return (forward, backward)


def per_device_wide(stem_tensor, stem_cotangent, branch_tensor, bit_order):
    members = lax.axis_size("stem")
    dev_bits = members.bit_length() - 1
    row_count, width = stem_tensor.shape
    local_size = row_count * width
    local_bits = local_size.bit_length() - 1
    free_size = local_size // members
    forward, backward = bit_tables(bit_order, local_bits, dev_bits)
    arranged = jnp.take(stem_tensor.reshape(local_size), backward).reshape(free_size, members)
    gathered = lax.all_gather(branch_tensor, "stem", axis=0, tiled=True)
    adjoint = lax.dot_general(
        stem_cotangent,
        gathered.astype(jnp.float32),
        (((1,), (1,)), ((), ())),
        precision=lax.Precision.HIGHEST,
        preferred_element_type=jnp.float32,
    )
    moved = lax.all_to_all(arranged, "stem", split_axis=1, concat_axis=1, tiled=True)
    returned = lax.all_to_all(adjoint.reshape(free_size, members), "stem", split_axis=1, concat_axis=1, tiled=True)
    perm_stem = moved.reshape(row_count, width)
    branch_term = lax.dot_general(
        perm_stem,
        stem_cotangent,
        (((0,), (0,)), ((), ())),
        precision=lax.Precision.HIGHEST,
        preferred_element_type=jnp.float32,
    )
    branch_grad = lax.psum_scatter(branch_term, "stem", scatter_dimension=0, tiled=True)
    stem_grad = jnp.take(returned.reshape(local_size), forward).reshape(row_count, width)
    return (stem_grad, branch_grad)


def split2(x):
    hi = x.astype(jnp.bfloat16)
    lo = (x - hi.astype(jnp.float32)).astype(jnp.bfloat16)
    return hi, lo


def dot(a, b):
    return jnp.dot(a, b, preferred_element_type=jnp.float32)


def dot_t(a, b):
    return lax.dot_general(a, b, (((1,), (1,)), ((), ())), preferred_element_type=jnp.float32)


def one_hot(index, rows):
    return (lax.broadcasted_iota(jnp.int32, (rows, index.shape[1]), 0) == index).astype(jnp.float32).astype(jnp.bfloat16)


def iota_row(size):
    return lax.broadcasted_iota(jnp.int32, (1, size), 1)


def permute_plan(pairs, rows):
    row_bits = rows.bit_length() - 1
    lane, row = iota_row(LANES), iota_row(rows)
    pre_lane, post_lane = jnp.zeros_like(lane), jnp.zeros_like(lane)
    pre_row, post_row = jnp.zeros_like(row), jnp.zeros_like(row)
    zero, one = jnp.int32(0), jnp.int32(1)
    moved_l, moved_r, kept_l, kept_r = zero, zero, zero, zero
    for i, o in pairs:
        i, o = jnp.int32(i), jnp.int32(o)
        li = jnp.where(i < LANE_BITS, one, zero)
        lo = jnp.where(o < LANE_BITS, one, zero)
        mid = jnp.where(
            li == 1,
            jnp.where(lo == 1, LANE_BITS - 1 - kept_l, moved_l),
            jnp.where(lo == 1, moved_r, row_bits - 1 - kept_r),
        )
        moved_l = moved_l + li * (1 - lo)
        moved_r = moved_r + (1 - li) * lo
        kept_l = kept_l + li * lo
        kept_r = kept_r + (1 - li) * (1 - lo)
        i_lane, i_row = i * li, (i - LANE_BITS) * (1 - li)
        o_lane, o_row = o * lo, (o - LANE_BITS) * (1 - lo)
        pre_lane = pre_lane + ((lane >> (mid * li)) & li) * (one << i_lane)
        pre_row = pre_row + ((row >> i_row) & (1 - li)) * (one << (mid * (1 - li)))
        post_lane = post_lane + ((lane >> o_lane) & lo) * (one << (mid * lo))
        post_row = post_row + ((row >> (mid * (1 - lo))) & (1 - lo)) * (one << o_row)
    return pre_lane, pre_row, post_lane, post_row, moved_l


def rows_times(m, x):
    hi, lo = split2(x)
    y = dot(m, jnp.concatenate([hi, lo], axis=1))
    return y[:, :LANES] + y[:, LANES:]


def lanes_times(x, m):
    hi, lo = split2(x)
    y = dot(jnp.concatenate([hi, lo], axis=0), m)
    return y[: x.shape[0]] + y[x.shape[0] :]


def permute_bits(x, plan):
    rows = x.shape[0]
    pre_lane, pre_row, post_lane, post_row, moved = plan
    x = lanes_times(x, one_hot(pre_lane, LANES))
    x = rows_times(one_hot(pre_row, rows), x)
    ri = lax.broadcasted_iota(jnp.int32, (rows, LANES), 0)
    ci = lax.broadcasted_iota(jnp.int32, (rows, LANES), 1)
    for s in range(LANE_BITS):
        step = 1 << s
        active = jnp.where(moved > s, jnp.int32(1), jnp.int32(0))
        up = pltpu.roll(pltpu.roll(x, rows - step, 0), step, 1)
        down = pltpu.roll(pltpu.roll(x, step, 0), LANES - step, 1)
        diff = (((ci >> s) & 1) - ((ri >> s) & 1)) * active
        x = jnp.where(diff == 1, up, jnp.where(diff == -1, down, x))
    x = rows_times(one_hot(post_row, rows), x)
    return lanes_times(x, one_hot(post_lane, LANES))


def encode(x, axis):
    top = jnp.maximum(jnp.max(jnp.abs(x), axis=axis, keepdims=True), 1e-30)
    return jnp.round(x * (CODES / top)).astype(jnp.int32).astype(jnp.int16), top * (1.0 / CODES)


def decode(q, step):
    return q.astype(jnp.int32).astype(jnp.float32) * step


def kernel(n, kinds, order, stem_hbm, cot_hbm, branch_hbm, stem_grad, branch_grad,
           stem, cot, branch, code, high, low, bsend, brecv, ssend, srecv, tsend, trecv,
           lsem, gss, grs, bss, brs, sss, srs, tss, trs):
    me = lax.axis_index("stem")
    rows, width = stem.shape
    tiles = width // LANES
    flat_rows = rows * tiles
    part = branch.shape[0] // n
    row_bits = rows.bit_length() - 1
    tile_bits = tiles.bit_length() - 1
    dev_bits = n.bit_length() - 1
    part_bits = part.bit_length() - 1
    local_bits = row_bits + tile_bits + LANE_BITS
    high_bits = local_bits - 2 * LANE_BITS
    cols = 2
    nz = n // cols
    z, x = me // cols, me % cols
    chunk = rows // len(kinds)
    targets = (jnp.minimum(me + cols, n - 1), jnp.maximum(me - cols, 0), z * cols + (1 - x))
    x_dev = targets[2]
    MESH = pl.DeviceIdType.MESH

    barrier = pltpu.get_barrier_semaphore()
    for off in range(1, n):
        pl.semaphore_signal(barrier, inc=1, device_id={"stem": (me + off) % n}, device_id_type=MESH)
    loads = [
        pltpu.make_async_copy(a, b, lsem.at[i])
        for i, (a, b) in enumerate(((stem_hbm, stem), (cot_hbm, cot), (branch_hbm, branch)))
    ]
    for load in loads:
        load.start()

    def held(i):
        return jnp.where(i < LANE_BITS, i, jnp.where(i < LANE_BITS + tile_bits, i + row_bits, i - tile_bits))

    def placed(p):
        if p < part_bits:
            return LANE_BITS + p
        if p < LANE_BITS:
            return local_bits - dev_bits + p - part_bits
        if p < 2 * LANE_BITS:
            return p - LANE_BITS
        return LANE_BITS + part_bits + p - 2 * LANE_BITS

    spots = [held(order[m]) for m in range(local_bits)]
    plan = permute_plan([(spots[m], placed(local_bits - 1 - m)) for m in range(local_bits)], flat_rows)

    loads[1].wait()
    q, step = encode(cot[...], 0)
    mine = pl.ds(pl.multiple_of(me * rows, rows), rows)
    code[mine, :] = q
    hi, lo = split2(cot[...])
    high[mine, :] = hi
    low[mine, :] = lo

    loads[2].wait()
    at = iota_row(n * part)
    pick = one_hot((at % n) * part + at // n, n * part)
    bsend[...] = dot(pick, branch[...]).astype(jnp.bfloat16).reshape(n, part, width)

    loads[0].wait()
    flat = jnp.concatenate([stem[:, t * LANES : (t + 1) * LANES] for t in range(tiles)], axis=0)
    arranged = permute_bits(flat, plan).reshape(n, flat_rows // n, LANES)
    ssend[...], stem_step = encode(arranged, 1)
    tsend[:, :, :width] = jnp.broadcast_to(step.reshape(1, 1, width), (n, 1, width))
    tsend[:, :, width:] = stem_step
    pl.semaphore_wait(barrier, n - 1)

    UP, DOWN, ACROSS = 0, 1, 2

    def block(c, o, way):
        place = code.at[pl.ds(pl.multiple_of(o * rows + c * chunk, chunk), chunk)]
        return pltpu.make_async_remote_copy(
            src_ref=place,
            dst_ref=place,
            send_sem=gss.at[c, o, way],
            recv_sem=grs.at[c, o],
            device_id={"stem": targets[way]},
            device_id_type=MESH,
        )

    def exists(way):
        return (z < nz - 1, z > 0, z >= 0)[way]

    def send(c, o, way):
        @pl.when(exists(way))
        def _():
            block(c, o, way).start()

    def arrive(c, o):
        block(c, o, ACROSS).wait_recv()

    def sent(c, o, way):
        @pl.when(exists(way))
        def _():
            block(c, o, way).wait_send()

    def direct(pair, off, incoming=False):
        src, dst, sems, rsems = pair
        peer = (me + off) % n
        origin = peer if incoming else me
        return pltpu.make_async_remote_copy(
            src_ref=src.at[peer],
            dst_ref=dst.at[origin],
            send_sem=sems.at[off],
            recv_sem=rsems.at[origin],
            device_id={"stem": peer},
            device_id_type=MESH,
        )

    branch_pair = (bsend, brecv, bss, brs)
    stem_pair = (ssend, srecv, sss, srs)
    step_pair = (tsend, trecv, tss, trs)

    for c in range(len(kinds)):
        for way in (UP, DOWN, ACROSS):
            send(c, me, way)
    for off in range(1, n):
        direct(step_pair, off).start()
    for off in range(1, n):
        direct(branch_pair, off).start()
    for off in range(1, n):
        direct(stem_pair, off).start()
    brecv[me] = bsend[me]
    srecv[me] = ssend[me]
    trecv[me] = tsend[me]

    def relay(act, k):
        for c, kind in enumerate(kinds):
            for xo in (x, 1 - x) if kind == "A" else (x,):
                for side, way in ((-k, UP), (k, DOWN)):
                    o = (z + side) * cols + xo

                    @pl.when((z + side >= 0) & (z + side <= nz - 1))
                    def _():
                        act(c, o, way)
                        if kind == "B":
                            act(c, o, ACROSS)

    def first(c, o, way):
        if way != ACROSS:
            arrive(c, o)
        send(c, o, way)

    for c, kind in enumerate(kinds):
        if kind == "A":
            arrive(c, x_dev)
            send(c, x_dev, UP)
            send(c, x_dev, DOWN)
    for k in range(1, nz):
        relay(first, k)
    for c, kind in enumerate(kinds):
        if kind == "B":
            for zz in range(nz):
                arrive(c, zz * cols + (1 - x))
    for off in range(1, n):
        direct(step_pair, off, True).wait_recv()
    for off in range(1, n):
        peer = (me + off) % n
        at = pl.ds(pl.multiple_of(peer * rows, rows), rows)
        hi, lo = split2(decode(code[at, :], trecv[peer][:, :width]))
        high[at, :] = hi
        low[at, :] = lo
    for off in range(1, n):
        direct(branch_pair, off, True).wait_recv()

    taken = brecv[...].reshape(n * part, width)
    adjoint = dot_t(high[...], taken) + dot_t(low[...], taken)
    plan = permute_plan([(local_bits - 1 - m, spots[m]) for m in range(local_bits)], flat_rows)
    back = permute_bits(adjoint, plan)
    for t in range(tiles):
        stem_grad[:, t * LANES : (t + 1) * LANES] = back[t * rows : (t + 1) * rows]

    for off in range(1, n):
        direct(stem_pair, off, True).wait_recv()
    highs = 1 << high_bits
    got = decode(srecv[...], trecv[:, :, width:])
    lhs = jnp.concatenate([got[:, e * part : (e + 1) * part].reshape(n * part, LANES) for e in range(highs)], axis=1)
    hi, lo = split2(lhs)
    at = iota_row(n * part)
    mix = one_hot((at % part) * n + at // part, n * part)
    hi = dot(mix, hi).astype(jnp.bfloat16)
    lo = dot(mix, lo).astype(jnp.bfloat16)
    branch_grad[...] = dot(hi, high[...]) + (dot(hi, low[...]) + dot(lo, high[...]))

    for pair in (step_pair, branch_pair, stem_pair):
        for off in range(1, n):
            direct(pair, off).wait_send()
    for c, kind in enumerate(kinds):
        for way in (UP, DOWN, ACROSS):
            sent(c, me, way)
        if kind == "A":
            sent(c, x_dev, UP)
            sent(c, x_dev, DOWN)
    for k in range(1, nz):
        relay(sent, k)


def per_device(stem_tensor, stem_cotangent, branch_tensor, bit_order):
    n = lax.axis_size("stem")
    rows, width = stem_tensor.shape
    flat_rows = rows * width // LANES
    if n != 8 or width != n * LANES or branch_tensor.shape[0] != LANES or (rows, flat_rows) != (64, 512):
        return per_device_wide(stem_tensor, stem_cotangent, branch_tensor, bit_order)
    part = branch_tensor.shape[0] // n
    vmem = pl.BlockSpec(memory_space=pltpu.VMEM)
    hbm = pl.BlockSpec(memory_space=pl.ANY)
    dma = pltpu.SemaphoreType.DMA
    return pl.pallas_call(
        functools.partial(kernel, n, KINDS),
        out_shape=(
            jax.ShapeDtypeStruct((rows, width), jnp.float32),
            jax.ShapeDtypeStruct(branch_tensor.shape, jnp.float32),
        ),
        in_specs=[pl.BlockSpec(memory_space=pltpu.SMEM), hbm, hbm, hbm],
        out_specs=(vmem, vmem),
        scratch_shapes=[
            pltpu.VMEM((rows, width), jnp.float32),
            pltpu.VMEM((rows, width), jnp.float32),
            pltpu.VMEM(branch_tensor.shape, jnp.bfloat16),
            pltpu.VMEM((n * rows, width), jnp.int16),
            pltpu.VMEM((n * rows, width), jnp.bfloat16),
            pltpu.VMEM((n * rows, width), jnp.bfloat16),
            pltpu.VMEM((n, part, width), jnp.bfloat16),
            pltpu.VMEM((n, part, width), jnp.bfloat16),
            pltpu.VMEM((n, flat_rows // n, LANES), jnp.int16),
            pltpu.VMEM((n, flat_rows // n, LANES), jnp.int16),
            pltpu.VMEM((n, 1, width + LANES), jnp.float32),
            pltpu.VMEM((n, 1, width + LANES), jnp.float32),
            dma((3,)),
            dma((len(KINDS), n, 3)),
            dma((len(KINDS), n)),
            dma((n,)),
            dma((n,)),
            dma((n,)),
            dma((n,)),
            dma((n,)),
            dma((n,)),
        ],
        compiler_params=pltpu.CompilerParams(
            collective_id=0, has_side_effects=True, vmem_limit_bytes=40 * 1024 * 1024
        ),
    )(bit_order, stem_tensor, stem_cotangent, branch_tensor)


def solution(mesh):
    placed = (P(("cuts", "stem"), None), P(("cuts", "stem"), None), P("stem", None), P())
    return jax.shard_map(
        per_device,
        mesh=mesh,
        in_specs=placed,
        out_specs=(P(("cuts", "stem"), None), P(("cuts", "stem"), None)),
        check_vma=False,
    )
```

```python
import functools

import jax
import jax.numpy as jnp
from jax import lax
from jax.experimental import pallas as pl
from jax.experimental.pallas import tpu as pltpu
from jax.sharding import PartitionSpec as P

LANES = 128
LANE_BITS = 7
CODES = 32767.0
KINDS = "BB"


def bit_tables(bit_order, local_bits, dev_bits):
    local_size = 2**local_bits
    positions = jnp.arange(local_size, dtype=jnp.int32)
    forward = jnp.zeros((local_size,), jnp.int32)
    backward = jnp.zeros((local_size,), jnp.int32)
    for order_pos in range(local_bits):
        if order_pos < dev_bits:
            target_bit = dev_bits - 1 - order_pos
        else:
            target_bit = dev_bits + local_bits - 1 - order_pos
        source = bit_order[order_pos]
        forward = forward + jnp.left_shift(jnp.right_shift(positions, source) & 1, target_bit)
        backward = backward + jnp.left_shift(jnp.right_shift(positions, target_bit) & 1, source)
    return (forward, backward)


def per_device_wide(stem_tensor, stem_cotangent, branch_tensor, bit_order):
    members = lax.axis_size("stem")
    dev_bits = members.bit_length() - 1
    row_count, width = stem_tensor.shape
    local_size = row_count * width
    local_bits = local_size.bit_length() - 1
    free_size = local_size // members
    forward, backward = bit_tables(bit_order, local_bits, dev_bits)
    arranged = jnp.take(stem_tensor.reshape(local_size), backward).reshape(free_size, members)
    gathered = lax.all_gather(branch_tensor, "stem", axis=0, tiled=True)
    adjoint = lax.dot_general(
        stem_cotangent,
        gathered.astype(jnp.float32),
        (((1,), (1,)), ((), ())),
        precision=lax.Precision.HIGHEST,
        preferred_element_type=jnp.float32,
    )
    moved = lax.all_to_all(arranged, "stem", split_axis=1, concat_axis=1, tiled=True)
    returned = lax.all_to_all(adjoint.reshape(free_size, members), "stem", split_axis=1, concat_axis=1, tiled=True)
    perm_stem = moved.reshape(row_count, width)
    branch_term = lax.dot_general(
        perm_stem,
        stem_cotangent,
        (((0,), (0,)), ((), ())),
        precision=lax.Precision.HIGHEST,
        preferred_element_type=jnp.float32,
    )
    branch_grad = lax.psum_scatter(branch_term, "stem", scatter_dimension=0, tiled=True)
    stem_grad = jnp.take(returned.reshape(local_size), forward).reshape(row_count, width)
    return (stem_grad, branch_grad)


def split2(x):
    hi = x.astype(jnp.bfloat16)
    lo = (x - hi.astype(jnp.float32)).astype(jnp.bfloat16)
    return hi, lo


def dot(a, b):
    return jnp.dot(a, b, preferred_element_type=jnp.float32)


def dot_t(a, b):
    return lax.dot_general(a, b, (((1,), (1,)), ((), ())), preferred_element_type=jnp.float32)


def one_hot(index, rows):
    return (lax.broadcasted_iota(jnp.int32, (rows, index.shape[1]), 0) == index).astype(jnp.float32).astype(jnp.bfloat16)


def iota_row(size):
    return lax.broadcasted_iota(jnp.int32, (1, size), 1)


def permute_plan(pairs, rows):
    row_bits = rows.bit_length() - 1
    lane, row = iota_row(LANES), iota_row(rows)
    pre_lane, post_lane = jnp.zeros_like(lane), jnp.zeros_like(lane)
    pre_row, post_row = jnp.zeros_like(row), jnp.zeros_like(row)
    zero, one = jnp.int32(0), jnp.int32(1)
    moved_l, moved_r, kept_l, kept_r = zero, zero, zero, zero
    for i, o in pairs:
        i, o = jnp.int32(i), jnp.int32(o)
        li = jnp.where(i < LANE_BITS, one, zero)
        lo = jnp.where(o < LANE_BITS, one, zero)
        on_lane = jnp.where(li == lo, LANE_BITS - 1 - kept_l, jnp.where(li == 1, moved_l, moved_r))
        on_row = jnp.where(li == lo, kept_r, row_bits - 1 - jnp.where(li == 1, moved_l, moved_r))
        moved_l = moved_l + li * (1 - lo)
        moved_r = moved_r + (1 - li) * lo
        kept_l = kept_l + li * lo
        kept_r = kept_r + (1 - li) * (1 - lo)
        i_lane, i_row = i * li, (i - LANE_BITS) * (1 - li)
        o_lane, o_row = o * lo, (o - LANE_BITS) * (1 - lo)
        pre_lane = pre_lane + ((lane >> (on_lane * li)) & li) * (one << i_lane)
        pre_row = pre_row + ((row >> i_row) & (1 - li)) * (one << (on_row * (1 - li)))
        post_lane = post_lane + ((lane >> o_lane) & lo) * (one << (on_lane * lo))
        post_row = post_row + ((row >> (on_row * (1 - lo))) & (1 - lo)) * (one << o_row)
    return pre_lane, pre_row, post_lane, post_row, moved_l


def rows_times(m, x):
    hi, lo = split2(x)
    y = dot(m, jnp.concatenate([hi, lo], axis=1))
    return y[:, :LANES] + y[:, LANES:]


def lanes_times(x, m):
    hi, lo = split2(x)
    y = dot(jnp.concatenate([hi, lo], axis=0), m)
    return y[: x.shape[0]] + y[x.shape[0] :]


def swap_bits(x, moved):
    rows = x.shape[0]
    row_bits = rows.bit_length() - 1
    lane = iota_row(LANES)
    for s in range(LANE_BITS):
        step = 1 << s
        group = 1 << (row_bits - 1 - s)
        active = jnp.where(moved > s, jnp.int32(1), jnp.int32(0))
        high = (lane >> s) & 1
        take_up = high * active == 1
        take_down = (1 - high) * active == 1
        if group >= 8:
            pairs = x.reshape(rows // (2 * group), 2, group, LANES)
            a = pairs[:, 0].reshape(rows // 2, LANES)
            b = pairs[:, 1].reshape(rows // 2, LANES)
            c = jnp.where(take_up, pltpu.roll(b, step, 1), a)
            d = jnp.where(take_down, pltpu.roll(a, LANES - step, 1), b)
            shape = (rows // (2 * group), 1, group, LANES)
            x = jnp.concatenate([c.reshape(shape), d.reshape(shape)], axis=1).reshape(rows, LANES)
        else:
            upper = (lax.broadcasted_iota(jnp.int32, (rows, 1), 0) // group) % 2
            up = pltpu.roll(pltpu.roll(x, rows - group, 0), step, 1)
            down = pltpu.roll(pltpu.roll(x, group, 0), LANES - step, 1)
            diff = (high - upper) * active
            x = jnp.where(diff == 1, up, jnp.where(diff == -1, down, x))
    return x


def permute_bits(x, plan, lanes_done=False):
    rows = x.shape[0]
    pre_lane, pre_row, post_lane, post_row, moved = plan
    if not lanes_done:
        x = lanes_times(x, one_hot(pre_lane, LANES))
    x = rows_times(one_hot(pre_row, rows), x)
    x = swap_bits(x, moved)
    x = rows_times(one_hot(post_row, rows), x)
    return lanes_times(x, one_hot(post_lane, LANES))


def encode(x, axis):
    top = jnp.maximum(jnp.max(jnp.abs(x), axis=axis, keepdims=True), 1e-30)
    return jnp.round(x * (CODES / top)).astype(jnp.int32).astype(jnp.int16), top * (1.0 / CODES)


def decode(q, step):
    return q.astype(jnp.int32).astype(jnp.float32) * step


def kernel(n, cuts, kinds, order, stem_hbm, cot_hbm, branch_hbm, stem_grad, branch_grad,
           stem, cot, branch, code, high, low, bsend, brecv, ssend, srecv, tsend, trecv,
           lsem, gss, grs, bss, brs, sss, srs, tss, trs, css, crs):
    me = lax.axis_index("stem")
    cut = lax.axis_index("cuts")
    rows, width = stem.shape
    tiles = width // LANES
    flat_rows = rows * tiles
    part = branch.shape[0] // n
    row_bits = rows.bit_length() - 1
    tile_bits = tiles.bit_length() - 1
    dev_bits = n.bit_length() - 1
    part_bits = part.bit_length() - 1
    local_bits = row_bits + tile_bits + LANE_BITS
    high_bits = local_bits - 2 * LANE_BITS
    cols = 2
    nz = n // cols
    z, x = me // cols, me % cols
    chunk = rows // len(kinds)
    targets = (jnp.minimum(me + cols, n - 1), jnp.maximum(me - cols, 0), z * cols + (1 - x))
    x_dev = targets[2]
    MESH = pl.DeviceIdType.MESH

    barrier = pltpu.get_barrier_semaphore()
    for off in range(1, n):
        pl.semaphore_signal(barrier, inc=1, device_id={"stem": (me + off) % n}, device_id_type=MESH)
    for off in range(1, cuts):
        pl.semaphore_signal(barrier, inc=1, device_id={"cuts": (cut + off) % cuts}, device_id_type=MESH)
    loads = [
        pltpu.make_async_copy(a, b, lsem.at[i])
        for i, (a, b) in enumerate(((stem_hbm, stem), (cot_hbm, cot), (branch_hbm, branch)))
    ]
    for load in loads:
        load.start()

    def held(i):
        return jnp.where(i < LANE_BITS, i, jnp.where(i < LANE_BITS + tile_bits, i + row_bits, i - tile_bits))

    def placed(p):
        if p < part_bits:
            return LANE_BITS + p
        if p < LANE_BITS:
            return local_bits - dev_bits + p - part_bits
        if p < 2 * LANE_BITS:
            return p - LANE_BITS
        return LANE_BITS + part_bits + p - 2 * LANE_BITS

    spots = [held(order[m]) for m in range(local_bits)]
    plan = permute_plan([(spots[m], placed(local_bits - 1 - m)) for m in range(local_bits)], flat_rows)

    loads[1].wait()
    q, step = encode(cot[...], 0)
    mine = pl.ds(pl.multiple_of(me * rows, rows), rows)
    code[mine, :] = q
    hi, lo = split2(cot[...])
    high[mine, :] = hi
    low[mine, :] = lo

    loads[2].wait()
    at = iota_row(n * part)
    pick = one_hot((at % n) * part + at // n, n * part)
    quarter = width // cuts
    columns = pl.ds(pl.multiple_of(cut * quarter, LANES), quarter)
    bsend[...] = dot(pick, branch[:, columns]).astype(jnp.bfloat16).reshape(n, part, quarter)

    loads[0].wait()
    flat = jnp.concatenate([stem[:, t * LANES : (t + 1) * LANES] for t in range(tiles)], axis=0)
    arranged = permute_bits(flat, plan).reshape(n, flat_rows // n, LANES)
    ssend[...], stem_step = encode(arranged, 1)
    tsend[:, :, :width] = jnp.broadcast_to(step.reshape(1, 1, width), (n, 1, width))
    tsend[:, :, width:] = stem_step
    pl.semaphore_wait(barrier, n - 1 + cuts - 1)

    UP, DOWN, ACROSS = 0, 1, 2

    def block(c, o, way):
        place = code.at[pl.ds(pl.multiple_of(o * rows + c * chunk, chunk), chunk)]
        return pltpu.make_async_remote_copy(
            src_ref=place,
            dst_ref=place,
            send_sem=gss.at[c, o, way],
            recv_sem=grs.at[c, o],
            device_id={"stem": targets[way]},
            device_id_type=MESH,
        )

    def exists(way):
        return (z < nz - 1, z > 0, z >= 0)[way]

    def send(c, o, way):
        @pl.when(exists(way))
        def _():
            block(c, o, way).start()

    def arrive(c, o):
        block(c, o, ACROSS).wait_recv()

    def sent(c, o, way):
        @pl.when(exists(way))
        def _():
            block(c, o, way).wait_send()

    def direct(pair, off, incoming=False):
        src, dst, sems, rsems = pair
        peer = (me + off) % n
        origin = peer if incoming else me
        return pltpu.make_async_remote_copy(
            src_ref=src.at[peer],
            dst_ref=dst.at[origin],
            send_sem=sems.at[off],
            recv_sem=rsems.at[origin],
            device_id={"stem": peer},
            device_id_type=MESH,
        )

    branch_pair = (bsend, brecv.at[cut], bss, brs)

    def share(off, incoming=False):
        origin = (cut + off) % cuts if incoming else cut
        return pltpu.make_async_remote_copy(
            src_ref=brecv.at[origin],
            dst_ref=brecv.at[origin],
            send_sem=css.at[off],
            recv_sem=crs.at[origin],
            device_id={"cuts": (cut + off) % cuts},
            device_id_type=MESH,
        )

    stem_pair = (ssend, srecv, sss, srs)
    step_pair = (tsend, trecv, tss, trs)

    for off in range(1, n):
        direct(branch_pair, off).start()
    for c in range(len(kinds)):
        for way in (UP, DOWN, ACROSS):
            send(c, me, way)
    for off in range(1, n):
        direct(step_pair, off).start()
    for off in range(1, n):
        direct(stem_pair, off).start()
    brecv[cut, me] = bsend[me]
    srecv[me] = ssend[me]
    trecv[me] = tsend[me]

    def relay(act, k):
        for c, kind in enumerate(kinds):
            for xo in (x, 1 - x) if kind == "A" else (x,):
                for side, way in ((-k, UP), (k, DOWN)):
                    o = (z + side) * cols + xo

                    @pl.when((z + side >= 0) & (z + side <= nz - 1))
                    def _():
                        act(c, o, way)
                        if kind == "B":
                            act(c, o, ACROSS)

    def first(c, o, way):
        if way != ACROSS:
            arrive(c, o)
        send(c, o, way)

    for c, kind in enumerate(kinds):
        if kind == "A":
            arrive(c, x_dev)
            send(c, x_dev, UP)
            send(c, x_dev, DOWN)
    relay(first, 1)
    for off in range(1, n):
        direct(branch_pair, off, True).wait_recv()
    for off in range(1, cuts):
        share(off).start()
    for k in range(2, nz):
        relay(first, k)

    def unpack(o):
        at = pl.ds(pl.multiple_of(o * rows, rows), rows)
        hi, lo = split2(decode(code[at, :], trecv[o][:, :width]))
        high[at, :] = hi
        low[at, :] = lo

    for off in range(1, n):
        direct(step_pair, off, True).wait_recv()
    for off in range(1, nz):
        unpack(((z + off) % nz) * cols + x)
    for off in range(1, cuts):
        share(off, True).wait_recv()
    plan = permute_plan([(local_bits - 1 - m, spots[m]) for m in range(local_bits)], flat_rows)
    lane_rows = one_hot(plan[0], LANES)
    taken = [
        lax.dot_general(
            lane_rows,
            brecv[e].reshape(n * part, quarter),
            (((0,), (0,)), ((), ())),
            preferred_element_type=jnp.float32,
        ).astype(jnp.bfloat16)
        for e in range(cuts)
    ]
    taken = jnp.concatenate(taken, axis=1)
    for off in range(1, n):
        direct(stem_pair, off, True).wait_recv()
    for off in range(nz):
        zz = (z + off) % nz
        for c, kind in enumerate(kinds):
            if kind == "B":
                arrive(c, zz * cols + (1 - x))
        unpack(zz * cols + (1 - x))

    adjoint = dot_t(high[...], taken) + dot_t(low[...], taken)
    back = permute_bits(adjoint, plan, True)
    for t in range(tiles):
        stem_grad[:, t * LANES : (t + 1) * LANES] = back[t * rows : (t + 1) * rows]

    highs = 1 << high_bits
    got = decode(srecv[...], trecv[:, :, width:])
    lhs = jnp.concatenate([got[:, e * part : (e + 1) * part].reshape(n * part, LANES) for e in range(highs)], axis=1)
    hi, lo = split2(lhs)
    at = iota_row(n * part)
    mix = one_hot((at % part) * n + at // part, n * part)
    hi = dot(mix, hi).astype(jnp.bfloat16)
    lo = dot(mix, lo).astype(jnp.bfloat16)
    branch_grad[...] = dot(hi, high[...]) + (dot(hi, low[...]) + dot(lo, high[...]))

    for off in range(1, cuts):
        share(off).wait_send()
    for pair in (step_pair, branch_pair, stem_pair):
        for off in range(1, n):
            direct(pair, off).wait_send()
    for c, kind in enumerate(kinds):
        for way in (UP, DOWN, ACROSS):
            sent(c, me, way)
        if kind == "A":
            sent(c, x_dev, UP)
            sent(c, x_dev, DOWN)
    for k in range(1, nz):
        relay(sent, k)


def per_device(stem_tensor, stem_cotangent, branch_tensor, bit_order):
    n, cuts = lax.axis_size("stem"), lax.axis_size("cuts")
    rows, width = stem_tensor.shape
    flat_rows = rows * width // LANES
    if n != 8 or width != n * LANES or branch_tensor.shape[0] != LANES or (rows, flat_rows) != (64, 512) or n % cuts:
        return per_device_wide(stem_tensor, stem_cotangent, branch_tensor, bit_order)
    part = branch_tensor.shape[0] // n
    vmem = pl.BlockSpec(memory_space=pltpu.VMEM)
    hbm = pl.BlockSpec(memory_space=pl.ANY)
    dma = pltpu.SemaphoreType.DMA
    return pl.pallas_call(
        functools.partial(kernel, n, cuts, KINDS),
        out_shape=(
            jax.ShapeDtypeStruct((rows, width), jnp.float32),
            jax.ShapeDtypeStruct(branch_tensor.shape, jnp.float32),
        ),
        in_specs=[pl.BlockSpec(memory_space=pltpu.SMEM), hbm, hbm, hbm],
        out_specs=(vmem, vmem),
        scratch_shapes=[
            pltpu.VMEM((rows, width), jnp.float32),
            pltpu.VMEM((rows, width), jnp.float32),
            pltpu.VMEM(branch_tensor.shape, jnp.bfloat16),
            pltpu.VMEM((n * rows, width), jnp.int16),
            pltpu.VMEM((n * rows, width), jnp.bfloat16),
            pltpu.VMEM((n * rows, width), jnp.bfloat16),
            pltpu.VMEM((n, part, width // cuts), jnp.bfloat16),
            pltpu.VMEM((cuts, n, part, width // cuts), jnp.bfloat16),
            pltpu.VMEM((n, flat_rows // n, LANES), jnp.int16),
            pltpu.VMEM((n, flat_rows // n, LANES), jnp.int16),
            pltpu.VMEM((n, 1, width + LANES), jnp.float32),
            pltpu.VMEM((n, 1, width + LANES), jnp.float32),
            dma((3,)),
            dma((len(KINDS), n, 3)),
            dma((len(KINDS), n)),
            dma((n,)),
            dma((n,)),
            dma((n,)),
            dma((n,)),
            dma((n,)),
            dma((n,)),
            dma((cuts,)),
            dma((cuts,)),
        ],
        compiler_params=pltpu.CompilerParams(
            collective_id=0, has_side_effects=True, vmem_limit_bytes=40 * 1024 * 1024
        ),
    )(bit_order, stem_tensor, stem_cotangent, branch_tensor)


def solution(mesh):
    placed = (P(("cuts", "stem"), None), P(("cuts", "stem"), None), P("stem", None), P())
    return jax.shard_map(
        per_device,
        mesh=mesh,
        in_specs=placed,
        out_specs=(P(("cuts", "stem"), None), P(("cuts", "stem"), None)),
        check_vma=False,
    )
```

```python
import functools

import jax
import jax.numpy as jnp
from jax import lax
from jax.experimental import pallas as pl
from jax.experimental.pallas import tpu as pltpu
from jax.sharding import PartitionSpec as P

LANES = 128
LANE_BITS = 7
CODES = 32767.0
KINDS = "BB"


def bit_tables(bit_order, local_bits, dev_bits):
    local_size = 2**local_bits
    positions = jnp.arange(local_size, dtype=jnp.int32)
    forward = jnp.zeros((local_size,), jnp.int32)
    backward = jnp.zeros((local_size,), jnp.int32)
    for order_pos in range(local_bits):
        if order_pos < dev_bits:
            target_bit = dev_bits - 1 - order_pos
        else:
            target_bit = dev_bits + local_bits - 1 - order_pos
        source = bit_order[order_pos]
        forward = forward + jnp.left_shift(jnp.right_shift(positions, source) & 1, target_bit)
        backward = backward + jnp.left_shift(jnp.right_shift(positions, target_bit) & 1, source)
    return (forward, backward)


def per_device_wide(stem_tensor, stem_cotangent, branch_tensor, bit_order):
    members = lax.axis_size("stem")
    dev_bits = members.bit_length() - 1
    row_count, width = stem_tensor.shape
    local_size = row_count * width
    local_bits = local_size.bit_length() - 1
    free_size = local_size // members
    forward, backward = bit_tables(bit_order, local_bits, dev_bits)
    arranged = jnp.take(stem_tensor.reshape(local_size), backward).reshape(free_size, members)
    gathered = lax.all_gather(branch_tensor, "stem", axis=0, tiled=True)
    adjoint = lax.dot_general(
        stem_cotangent,
        gathered.astype(jnp.float32),
        (((1,), (1,)), ((), ())),
        precision=lax.Precision.HIGHEST,
        preferred_element_type=jnp.float32,
    )
    moved = lax.all_to_all(arranged, "stem", split_axis=1, concat_axis=1, tiled=True)
    returned = lax.all_to_all(adjoint.reshape(free_size, members), "stem", split_axis=1, concat_axis=1, tiled=True)
    perm_stem = moved.reshape(row_count, width)
    branch_term = lax.dot_general(
        perm_stem,
        stem_cotangent,
        (((0,), (0,)), ((), ())),
        precision=lax.Precision.HIGHEST,
        preferred_element_type=jnp.float32,
    )
    branch_grad = lax.psum_scatter(branch_term, "stem", scatter_dimension=0, tiled=True)
    stem_grad = jnp.take(returned.reshape(local_size), forward).reshape(row_count, width)
    return (stem_grad, branch_grad)


def split2(x):
    hi = x.astype(jnp.bfloat16)
    lo = (x - hi.astype(jnp.float32)).astype(jnp.bfloat16)
    return hi, lo


def dot(a, b):
    return jnp.dot(a, b, preferred_element_type=jnp.float32)


def dot_t(a, b):
    return lax.dot_general(a, b, (((1,), (1,)), ((), ())), preferred_element_type=jnp.float32)


def one_hot(index, rows):
    return (lax.broadcasted_iota(jnp.int32, (rows, index.shape[1]), 0) == index).astype(jnp.float32).astype(jnp.bfloat16)


def iota_row(size):
    return lax.broadcasted_iota(jnp.int32, (1, size), 1)


def permute_plan(pairs, rows):
    row_bits = rows.bit_length() - 1
    lane, row = iota_row(LANES), iota_row(rows)
    pre_lane, post_lane = jnp.zeros_like(lane), jnp.zeros_like(lane)
    pre_row, post_row = jnp.zeros_like(row), jnp.zeros_like(row)
    zero, one = jnp.int32(0), jnp.int32(1)
    moved_l, moved_r, kept_l, kept_r = zero, zero, zero, zero
    for i, o in pairs:
        i, o = jnp.int32(i), jnp.int32(o)
        li = jnp.where(i < LANE_BITS, one, zero)
        lo = jnp.where(o < LANE_BITS, one, zero)
        on_lane = jnp.where(li == lo, LANE_BITS - 1 - kept_l, jnp.where(li == 1, moved_l, moved_r))
        on_row = jnp.where(li == lo, kept_r, row_bits - 1 - jnp.where(li == 1, moved_l, moved_r))
        moved_l = moved_l + li * (1 - lo)
        moved_r = moved_r + (1 - li) * lo
        kept_l = kept_l + li * lo
        kept_r = kept_r + (1 - li) * (1 - lo)
        i_lane, i_row = i * li, (i - LANE_BITS) * (1 - li)
        o_lane, o_row = o * lo, (o - LANE_BITS) * (1 - lo)
        pre_lane = pre_lane + ((lane >> (on_lane * li)) & li) * (one << i_lane)
        pre_row = pre_row + ((row >> i_row) & (1 - li)) * (one << (on_row * (1 - li)))
        post_lane = post_lane + ((lane >> o_lane) & lo) * (one << (on_lane * lo))
        post_row = post_row + ((row >> (on_row * (1 - lo))) & (1 - lo)) * (one << o_row)
    return pre_lane, pre_row, post_lane, post_row, moved_l


def rows_times(m, x):
    hi, lo = split2(x)
    y = dot(m, jnp.concatenate([hi, lo], axis=1))
    return y[:, :LANES] + y[:, LANES:]


def lanes_times(x, m):
    hi, lo = split2(x)
    y = dot(jnp.concatenate([hi, lo], axis=0), m)
    return y[: x.shape[0]] + y[x.shape[0] :]


def swap_bits(x, moved):
    rows = x.shape[0]
    row_bits = rows.bit_length() - 1
    lane = iota_row(LANES)
    for s in range(LANE_BITS):
        step = 1 << s
        group = 1 << (row_bits - 1 - s)
        active = jnp.where(moved > s, jnp.int32(1), jnp.int32(0))
        high = (lane >> s) & 1
        take_up = high * active == 1
        take_down = (1 - high) * active == 1
        if group >= 8:
            pairs = x.reshape(rows // (2 * group), 2, group, LANES)
            a = pairs[:, 0].reshape(rows // 2, LANES)
            b = pairs[:, 1].reshape(rows // 2, LANES)
            c = jnp.where(take_up, pltpu.roll(b, step, 1), a)
            d = jnp.where(take_down, pltpu.roll(a, LANES - step, 1), b)
            shape = (rows // (2 * group), 1, group, LANES)
            x = jnp.concatenate([c.reshape(shape), d.reshape(shape)], axis=1).reshape(rows, LANES)
        else:
            upper = (lax.broadcasted_iota(jnp.int32, (rows, 1), 0) // group) % 2
            up = pltpu.roll(pltpu.roll(x, rows - group, 0), step, 1)
            down = pltpu.roll(pltpu.roll(x, group, 0), LANES - step, 1)
            diff = (high - upper) * active
            x = jnp.where(diff == 1, up, jnp.where(diff == -1, down, x))
    return x


def permute_bits(x, plan):
    rows = x.shape[0]
    pre_lane, pre_row, post_lane, post_row, moved = plan
    x = lanes_times(x, one_hot(pre_lane, LANES))
    x = rows_times(one_hot(pre_row, rows), x)
    x = swap_bits(x, moved)
    x = rows_times(one_hot(post_row, rows), x)
    return lanes_times(x, one_hot(post_lane, LANES))


def encode(x, axis):
    top = jnp.maximum(jnp.max(jnp.abs(x), axis=axis, keepdims=True), 1e-30)
    return jnp.round(x * (CODES / top)).astype(jnp.int32).astype(jnp.int16), top * (1.0 / CODES)


def decode(q, step):
    return q.astype(jnp.int32).astype(jnp.float32) * step


def kernel(n, cuts, kinds, order, stem_hbm, cot_hbm, branch_hbm, stem_grad, branch_grad,
           stem, cot, branch, code, high, low, bsend, brecv, ssend, srecv, tsend, trecv,
           lsem, gss, grs, bss, brs, sss, srs, tss, trs, css, crs, adj, first_rows, last_rows):
    me = lax.axis_index("stem")
    cut = lax.axis_index("cuts")
    rows, width = stem.shape
    tiles = width // LANES
    flat_rows = rows * tiles
    part = branch.shape[0] // n
    row_bits = rows.bit_length() - 1
    tile_bits = tiles.bit_length() - 1
    dev_bits = n.bit_length() - 1
    part_bits = part.bit_length() - 1
    local_bits = row_bits + tile_bits + LANE_BITS
    high_bits = local_bits - 2 * LANE_BITS
    cols = 2
    nz = n // cols
    z, x = me // cols, me % cols
    chunk = rows // len(kinds)
    targets = (jnp.minimum(me + cols, n - 1), jnp.maximum(me - cols, 0), z * cols + (1 - x))
    x_dev = targets[2]
    MESH = pl.DeviceIdType.MESH

    barrier = pltpu.get_barrier_semaphore()
    for off in range(1, n):
        pl.semaphore_signal(barrier, inc=1, device_id={"stem": (me + off) % n}, device_id_type=MESH)
    for off in range(1, cuts):
        pl.semaphore_signal(barrier, inc=1, device_id={"cuts": (cut + off) % cuts}, device_id_type=MESH)
    loads = [
        pltpu.make_async_copy(a, b, lsem.at[i])
        for i, (a, b) in enumerate(((stem_hbm, stem), (cot_hbm, cot), (branch_hbm, branch)))
    ]
    for load in loads:
        load.start()

    def held(i):
        return jnp.where(i < LANE_BITS, i, jnp.where(i < LANE_BITS + tile_bits, i + row_bits, i - tile_bits))

    def placed(p):
        if p < part_bits:
            return LANE_BITS + p
        if p < LANE_BITS:
            return local_bits - dev_bits + p - part_bits
        if p < 2 * LANE_BITS:
            return p - LANE_BITS
        return LANE_BITS + part_bits + p - 2 * LANE_BITS

    spots = [held(order[m]) for m in range(local_bits)]
    plan = permute_plan([(spots[m], placed(local_bits - 1 - m)) for m in range(local_bits)], flat_rows)

    loads[1].wait()
    q, step = encode(cot[...], 0)
    mine = pl.ds(pl.multiple_of(me * rows, rows), rows)
    code[mine, :] = q
    hi, lo = split2(cot[...])
    high[mine, :] = hi
    low[mine, :] = lo

    loads[2].wait()
    at = iota_row(n * part)
    pick = one_hot((at % n) * part + at // n, n * part)
    quarter = width // cuts
    columns = pl.ds(pl.multiple_of(cut * quarter, LANES), quarter)
    bsend[...] = dot(pick, branch[:, columns]).astype(jnp.bfloat16).reshape(n, part, quarter)

    loads[0].wait()
    flat = jnp.concatenate([stem[:, t * LANES : (t + 1) * LANES] for t in range(tiles)], axis=0)
    arranged = permute_bits(flat, plan).reshape(n, flat_rows // n, LANES)
    ssend[...], stem_step = encode(arranged, 1)
    tsend[:, :, :width] = jnp.broadcast_to(step.reshape(1, 1, width), (n, 1, width))
    tsend[:, :, width:] = stem_step
    pl.semaphore_wait(barrier, n - 1 + cuts - 1)

    UP, DOWN, ACROSS = 0, 1, 2

    def block(c, o, way):
        place = code.at[pl.ds(pl.multiple_of(o * rows + c * chunk, chunk), chunk)]
        return pltpu.make_async_remote_copy(
            src_ref=place,
            dst_ref=place,
            send_sem=gss.at[c, o, way],
            recv_sem=grs.at[c, o],
            device_id={"stem": targets[way]},
            device_id_type=MESH,
        )

    def exists(way):
        return (z < nz - 1, z > 0, z >= 0)[way]

    def send(c, o, way):
        @pl.when(exists(way))
        def _():
            block(c, o, way).start()

    def arrive(c, o):
        block(c, o, ACROSS).wait_recv()

    def sent(c, o, way):
        @pl.when(exists(way))
        def _():
            block(c, o, way).wait_send()

    def direct(pair, off, incoming=False):
        src, dst, sems, rsems = pair
        peer = (me + off) % n
        origin = peer if incoming else me
        return pltpu.make_async_remote_copy(
            src_ref=src.at[peer],
            dst_ref=dst.at[origin],
            send_sem=sems.at[off],
            recv_sem=rsems.at[origin],
            device_id={"stem": peer},
            device_id_type=MESH,
        )

    branch_pair = (bsend, brecv.at[cut], bss, brs)

    def share(off, incoming=False):
        origin = (cut + off) % cuts if incoming else cut
        return pltpu.make_async_remote_copy(
            src_ref=brecv.at[origin],
            dst_ref=brecv.at[origin],
            send_sem=css.at[off],
            recv_sem=crs.at[origin],
            device_id={"cuts": (cut + off) % cuts},
            device_id_type=MESH,
        )

    stem_pair = (ssend, srecv, sss, srs)
    step_pair = (tsend, trecv, tss, trs)

    for off in range(1, n):
        direct(branch_pair, off).start()
    for c in range(len(kinds)):
        for way in (UP, DOWN, ACROSS):
            send(c, me, way)
    for off in range(1, n):
        direct(step_pair, off).start()
    for off in range(1, n):
        direct(stem_pair, off).start()
    brecv[cut, me] = bsend[me]
    srecv[me] = ssend[me]
    trecv[me] = tsend[me]

    def relay(act, k):
        for c, kind in enumerate(kinds):
            for xo in (x, 1 - x) if kind == "A" else (x,):
                for side, way in ((-k, UP), (k, DOWN)):
                    o = (z + side) * cols + xo

                    @pl.when((z + side >= 0) & (z + side <= nz - 1))
                    def _():
                        act(c, o, way)
                        if kind == "B":
                            act(c, o, ACROSS)

    def first(c, o, way):
        if way != ACROSS:
            arrive(c, o)
        send(c, o, way)

    for c, kind in enumerate(kinds):
        if kind == "A":
            arrive(c, x_dev)
            send(c, x_dev, UP)
            send(c, x_dev, DOWN)
    relay(first, 1)
    for off in range(1, n):
        direct(branch_pair, off, True).wait_recv()
    for off in range(1, cuts):
        share(off).start()
    for k in range(2, nz):
        relay(first, k)

    def unpack(o):
        at = pl.ds(pl.multiple_of(o * rows, rows), rows)
        hi, lo = split2(decode(code[at, :], trecv[o][:, :width]))
        high[at, :] = hi
        low[at, :] = lo

    for off in range(1, n):
        direct(step_pair, off, True).wait_recv()
    for off in range(1, nz):
        unpack(((z + off) % nz) * cols + x)
    for off in range(1, cuts):
        share(off, True).wait_recv()
    plan = permute_plan([(local_bits - 1 - m, spots[m]) for m in range(local_bits)], flat_rows)
    lane_rows = one_hot(plan[0], LANES)
    first_rows[...] = one_hot(plan[1], flat_rows)
    last_rows[...] = one_hot(plan[3], flat_rows)
    last_lanes = one_hot(plan[2], LANES)
    taken = [
        lax.dot_general(
            lane_rows,
            brecv[e].reshape(n * part, quarter),
            (((0,), (0,)), ((), ())),
            preferred_element_type=jnp.float32,
        ).astype(jnp.bfloat16)
        for e in range(cuts)
    ]
    taken = jnp.concatenate(taken, axis=1)
    for off in range(1, n):
        direct(stem_pair, off, True).wait_recv()
    highs = 1 << high_bits
    got = decode(srecv[...], trecv[:, :, width:])
    lhs = jnp.concatenate([got[:, e * part : (e + 1) * part].reshape(n * part, LANES) for e in range(highs)], axis=1)
    hi, lo = split2(lhs)
    at = iota_row(n * part)
    mix = one_hot((at % part) * n + at // part, n * part)
    left_hi = dot(mix, hi).astype(jnp.bfloat16)
    left_lo = dot(mix, lo).astype(jnp.bfloat16)

    def adjoin(o):
        at = pl.ds(pl.multiple_of(o * rows, rows), rows)
        both = dot_t(jnp.concatenate([high[at, :], low[at, :]], axis=0), taken)
        adj[at, :] = both[:rows] + both[rows:]

    for off in range(nz):
        adjoin(((z + off) % nz) * cols + x)
    for off in range(nz):
        zz = (z + off) % nz
        for c, kind in enumerate(kinds):
            if kind == "B":
                arrive(c, zz * cols + (1 - x))
        unpack(zz * cols + (1 - x))
        adjoin(zz * cols + (1 - x))

    back = swap_bits(rows_times(first_rows[...], adj[...]), plan[4])
    back = lanes_times(rows_times(last_rows[...], back), last_lanes)
    for t in range(tiles):
        stem_grad[:, t * LANES : (t + 1) * LANES] = back[t * rows : (t + 1) * rows]

    branch_grad[...] = dot(left_hi, high[...]) + (dot(left_hi, low[...]) + dot(left_lo, high[...]))

    for off in range(1, cuts):
        share(off).wait_send()
    for pair in (step_pair, branch_pair, stem_pair):
        for off in range(1, n):
            direct(pair, off).wait_send()
    for c, kind in enumerate(kinds):
        for way in (UP, DOWN, ACROSS):
            sent(c, me, way)
        if kind == "A":
            sent(c, x_dev, UP)
            sent(c, x_dev, DOWN)
    for k in range(1, nz):
        relay(sent, k)


def per_device(stem_tensor, stem_cotangent, branch_tensor, bit_order):
    n, cuts = lax.axis_size("stem"), lax.axis_size("cuts")
    rows, width = stem_tensor.shape
    flat_rows = rows * width // LANES
    if n != 8 or width != n * LANES or branch_tensor.shape[0] != LANES or (rows, flat_rows) != (64, 512) or n % cuts:
        return per_device_wide(stem_tensor, stem_cotangent, branch_tensor, bit_order)
    part = branch_tensor.shape[0] // n
    vmem = pl.BlockSpec(memory_space=pltpu.VMEM)
    hbm = pl.BlockSpec(memory_space=pl.ANY)
    dma = pltpu.SemaphoreType.DMA
    return pl.pallas_call(
        functools.partial(kernel, n, cuts, KINDS),
        out_shape=(
            jax.ShapeDtypeStruct((rows, width), jnp.float32),
            jax.ShapeDtypeStruct(branch_tensor.shape, jnp.float32),
        ),
        in_specs=[pl.BlockSpec(memory_space=pltpu.SMEM), hbm, hbm, hbm],
        out_specs=(vmem, vmem),
        scratch_shapes=[
            pltpu.VMEM((rows, width), jnp.float32),
            pltpu.VMEM((rows, width), jnp.float32),
            pltpu.VMEM(branch_tensor.shape, jnp.bfloat16),
            pltpu.VMEM((n * rows, width), jnp.int16),
            pltpu.VMEM((n * rows, width), jnp.bfloat16),
            pltpu.VMEM((n * rows, width), jnp.bfloat16),
            pltpu.VMEM((n, part, width // cuts), jnp.bfloat16),
            pltpu.VMEM((cuts, n, part, width // cuts), jnp.bfloat16),
            pltpu.VMEM((n, flat_rows // n, LANES), jnp.int16),
            pltpu.VMEM((n, flat_rows // n, LANES), jnp.int16),
            pltpu.VMEM((n, 1, width + LANES), jnp.float32),
            pltpu.VMEM((n, 1, width + LANES), jnp.float32),
            dma((3,)),
            dma((len(KINDS), n, 3)),
            dma((len(KINDS), n)),
            dma((n,)),
            dma((n,)),
            dma((n,)),
            dma((n,)),
            dma((n,)),
            dma((n,)),
            dma((cuts,)),
            dma((cuts,)),
            pltpu.VMEM((flat_rows, LANES), jnp.float32),
            pltpu.VMEM((flat_rows, flat_rows), jnp.bfloat16),
            pltpu.VMEM((flat_rows, flat_rows), jnp.bfloat16),
        ],
        compiler_params=pltpu.CompilerParams(
            collective_id=0, has_side_effects=True, vmem_limit_bytes=40 * 1024 * 1024
        ),
    )(bit_order, stem_tensor, stem_cotangent, branch_tensor)


def solution(mesh):
    placed = (P(("cuts", "stem"), None), P(("cuts", "stem"), None), P("stem", None), P())
    return jax.shard_map(
        per_device,
        mesh=mesh,
        in_specs=placed,
        out_specs=(P(("cuts", "stem"), None), P(("cuts", "stem"), None)),
        check_vma=False,
    )
```

```python
import functools

import jax
import jax.numpy as jnp
from jax import lax
from jax.experimental import pallas as pl
from jax.experimental.pallas import tpu as pltpu
from jax.sharding import PartitionSpec as P

LANES = 128
LANE_BITS = 7
CODES = 32767.0
KINDS = "BB"


def bit_tables(bit_order, local_bits, dev_bits):
    local_size = 2**local_bits
    positions = jnp.arange(local_size, dtype=jnp.int32)
    forward = jnp.zeros((local_size,), jnp.int32)
    backward = jnp.zeros((local_size,), jnp.int32)
    for order_pos in range(local_bits):
        if order_pos < dev_bits:
            target_bit = dev_bits - 1 - order_pos
        else:
            target_bit = dev_bits + local_bits - 1 - order_pos
        source = bit_order[order_pos]
        forward = forward + jnp.left_shift(jnp.right_shift(positions, source) & 1, target_bit)
        backward = backward + jnp.left_shift(jnp.right_shift(positions, target_bit) & 1, source)
    return (forward, backward)


def per_device_wide(stem_tensor, stem_cotangent, branch_tensor, bit_order):
    members = lax.axis_size("stem")
    dev_bits = members.bit_length() - 1
    row_count, width = stem_tensor.shape
    local_size = row_count * width
    local_bits = local_size.bit_length() - 1
    free_size = local_size // members
    forward, backward = bit_tables(bit_order, local_bits, dev_bits)
    arranged = jnp.take(stem_tensor.reshape(local_size), backward).reshape(free_size, members)
    gathered = lax.all_gather(branch_tensor, "stem", axis=0, tiled=True)
    adjoint = lax.dot_general(
        stem_cotangent,
        gathered.astype(jnp.float32),
        (((1,), (1,)), ((), ())),
        precision=lax.Precision.HIGHEST,
        preferred_element_type=jnp.float32,
    )
    moved = lax.all_to_all(arranged, "stem", split_axis=1, concat_axis=1, tiled=True)
    returned = lax.all_to_all(adjoint.reshape(free_size, members), "stem", split_axis=1, concat_axis=1, tiled=True)
    perm_stem = moved.reshape(row_count, width)
    branch_term = lax.dot_general(
        perm_stem,
        stem_cotangent,
        (((0,), (0,)), ((), ())),
        precision=lax.Precision.HIGHEST,
        preferred_element_type=jnp.float32,
    )
    branch_grad = lax.psum_scatter(branch_term, "stem", scatter_dimension=0, tiled=True)
    stem_grad = jnp.take(returned.reshape(local_size), forward).reshape(row_count, width)
    return (stem_grad, branch_grad)


def split2(x):
    hi = x.astype(jnp.bfloat16)
    lo = (x - hi.astype(jnp.float32)).astype(jnp.bfloat16)
    return hi, lo


def dot(a, b):
    return jnp.dot(a, b, preferred_element_type=jnp.float32)


def dot_t(a, b):
    return lax.dot_general(a, b, (((1,), (1,)), ((), ())), preferred_element_type=jnp.float32)


def one_hot(index, rows):
    return (lax.broadcasted_iota(jnp.int32, (rows, index.shape[1]), 0) == index).astype(jnp.float32).astype(jnp.bfloat16)


def iota_row(size):
    return lax.broadcasted_iota(jnp.int32, (1, size), 1)


def permute_plan(pairs, rows):
    row_bits = rows.bit_length() - 1
    lane, row = iota_row(LANES), iota_row(rows)
    pre_lane, post_lane = jnp.zeros_like(lane), jnp.zeros_like(lane)
    pre_row, post_row = jnp.zeros_like(row), jnp.zeros_like(row)
    zero, one = jnp.int32(0), jnp.int32(1)
    moved_l, moved_r, kept_l, kept_r = zero, zero, zero, zero
    for i, o in pairs:
        i, o = jnp.int32(i), jnp.int32(o)
        li = jnp.where(i < LANE_BITS, one, zero)
        lo = jnp.where(o < LANE_BITS, one, zero)
        on_lane = jnp.where(li == lo, LANE_BITS - 1 - kept_l, jnp.where(li == 1, moved_l, moved_r))
        on_row = jnp.where(li == lo, kept_r, row_bits - 1 - jnp.where(li == 1, moved_l, moved_r))
        moved_l = moved_l + li * (1 - lo)
        moved_r = moved_r + (1 - li) * lo
        kept_l = kept_l + li * lo
        kept_r = kept_r + (1 - li) * (1 - lo)
        i_lane, i_row = i * li, (i - LANE_BITS) * (1 - li)
        o_lane, o_row = o * lo, (o - LANE_BITS) * (1 - lo)
        pre_lane = pre_lane + ((lane >> (on_lane * li)) & li) * (one << i_lane)
        pre_row = pre_row + ((row >> i_row) & (1 - li)) * (one << (on_row * (1 - li)))
        post_lane = post_lane + ((lane >> o_lane) & lo) * (one << (on_lane * lo))
        post_row = post_row + ((row >> (on_row * (1 - lo))) & (1 - lo)) * (one << o_row)
    return pre_lane, pre_row, post_lane, post_row, moved_l


def rows_times(m, x):
    hi, lo = split2(x)
    y = dot(m, jnp.concatenate([hi, lo], axis=1))
    return y[:, :LANES] + y[:, LANES:]


def lanes_times(x, m):
    hi, lo = split2(x)
    y = dot(jnp.concatenate([hi, lo], axis=0), m)
    return y[: x.shape[0]] + y[x.shape[0] :]


def swap_bits(x, moved):
    rows = x.shape[0]
    row_bits = rows.bit_length() - 1
    lane = iota_row(LANES)
    for s in range(LANE_BITS):
        step = 1 << s
        group = 1 << (row_bits - 1 - s)
        active = jnp.where(moved > s, jnp.int32(1), jnp.int32(0))
        high = (lane >> s) & 1
        take_up = high * active == 1
        take_down = (1 - high) * active == 1
        if group >= 8:
            pairs = x.reshape(rows // (2 * group), 2, group, LANES)
            a = pairs[:, 0].reshape(rows // 2, LANES)
            b = pairs[:, 1].reshape(rows // 2, LANES)
            c = jnp.where(take_up, pltpu.roll(b, step, 1), a)
            d = jnp.where(take_down, pltpu.roll(a, LANES - step, 1), b)
            shape = (rows // (2 * group), 1, group, LANES)
            x = jnp.concatenate([c.reshape(shape), d.reshape(shape)], axis=1).reshape(rows, LANES)
        else:
            upper = (lax.broadcasted_iota(jnp.int32, (rows, 1), 0) // group) % 2
            up = pltpu.roll(pltpu.roll(x, rows - group, 0), step, 1)
            down = pltpu.roll(pltpu.roll(x, group, 0), LANES - step, 1)
            diff = (high - upper) * active
            x = jnp.where(diff == 1, up, jnp.where(diff == -1, down, x))
    return x


def permute_bits(x, plan):
    rows = x.shape[0]
    pre_lane, pre_row, post_lane, post_row, moved = plan
    x = lanes_times(x, one_hot(pre_lane, LANES))
    x = rows_times(one_hot(pre_row, rows), x)
    x = swap_bits(x, moved)
    x = rows_times(one_hot(post_row, rows), x)
    return lanes_times(x, one_hot(post_lane, LANES))


def encode(x, axis):
    top = jnp.maximum(jnp.max(jnp.abs(x), axis=axis, keepdims=True), 1e-30)
    return jnp.round(x * (CODES / top)).astype(jnp.int32).astype(jnp.int16), top * (1.0 / CODES)


def decode(q, step):
    return q.astype(jnp.int32).astype(jnp.float32) * step


def kernel(n, cuts, kinds, order, stem_hbm, cot_hbm, branch_hbm, stem_grad, branch_grad,
           stem, cot, branch, code, high, low, bsend, brecv, ssend, srecv, tsend, trecv,
           lsem, gss, grs, bss, brs, sss, srs, tss, trs, css, crs, adj, first_rows, last_rows):
    me = lax.axis_index("stem")
    cut = lax.axis_index("cuts")
    rows, width = stem.shape
    tiles = width // LANES
    flat_rows = rows * tiles
    part = branch.shape[0] // n
    row_bits = rows.bit_length() - 1
    tile_bits = tiles.bit_length() - 1
    dev_bits = n.bit_length() - 1
    part_bits = part.bit_length() - 1
    local_bits = row_bits + tile_bits + LANE_BITS
    high_bits = local_bits - 2 * LANE_BITS
    cols = 2
    nz = n // cols
    z, x = me // cols, me % cols
    chunk = rows // len(kinds)
    targets = (jnp.minimum(me + cols, n - 1), jnp.maximum(me - cols, 0), z * cols + (1 - x))
    x_dev = targets[2]
    MESH = pl.DeviceIdType.MESH

    barrier = pltpu.get_barrier_semaphore()
    for off in range(1, n):
        pl.semaphore_signal(barrier, inc=1, device_id={"stem": (me + off) % n}, device_id_type=MESH)
    for off in range(1, cuts):
        pl.semaphore_signal(barrier, inc=1, device_id={"cuts": (cut + off) % cuts}, device_id_type=MESH)
    loads = [
        pltpu.make_async_copy(a, b, lsem.at[i])
        for i, (a, b) in enumerate(((stem_hbm, stem), (cot_hbm, cot), (branch_hbm, branch)))
    ]
    for load in loads:
        load.start()

    def held(i):
        return jnp.where(i < LANE_BITS, i, jnp.where(i < LANE_BITS + tile_bits, i + row_bits, i - tile_bits))

    def placed(p):
        if p < part_bits:
            return LANE_BITS + p
        if p < LANE_BITS:
            return local_bits - dev_bits + p - part_bits
        if p < 2 * LANE_BITS:
            return p - LANE_BITS
        return LANE_BITS + part_bits + p - 2 * LANE_BITS

    spots = [held(order[m]) for m in range(local_bits)]
    plan = permute_plan([(spots[m], placed(local_bits - 1 - m)) for m in range(local_bits)], flat_rows)

    loads[1].wait()
    q, step = encode(cot[...], 0)
    mine = pl.ds(pl.multiple_of(me * rows, rows), rows)
    code[mine, :] = q
    hi, lo = split2(cot[...])
    high[mine, :] = hi
    low[mine, :] = lo

    loads[2].wait()
    at = iota_row(n * part)
    pick = one_hot((at % n) * part + at // n, n * part)
    quarter = width // cuts
    columns = pl.ds(pl.multiple_of(cut * quarter, LANES), quarter)
    bsend[...] = dot(pick, branch[:, columns]).astype(jnp.bfloat16).reshape(n, part, quarter)

    UP, DOWN, ACROSS = 0, 1, 2

    def block(c, o, way):
        place = code.at[pl.ds(pl.multiple_of(o * rows + c * chunk, chunk), chunk)]
        return pltpu.make_async_remote_copy(
            src_ref=place,
            dst_ref=place,
            send_sem=gss.at[c, o, way],
            recv_sem=grs.at[c, o],
            device_id={"stem": targets[way]},
            device_id_type=MESH,
        )

    def exists(way):
        return (z < nz - 1, z > 0, z >= 0)[way]

    def send(c, o, way):
        @pl.when(exists(way))
        def _():
            block(c, o, way).start()

    def arrive(c, o):
        block(c, o, ACROSS).wait_recv()

    def sent(c, o, way):
        @pl.when(exists(way))
        def _():
            block(c, o, way).wait_send()

    def direct(pair, off, incoming=False):
        src, dst, sems, rsems = pair
        peer = (me + off) % n
        origin = peer if incoming else me
        return pltpu.make_async_remote_copy(
            src_ref=src.at[peer],
            dst_ref=dst.at[origin],
            send_sem=sems.at[off],
            recv_sem=rsems.at[origin],
            device_id={"stem": peer},
            device_id_type=MESH,
        )

    branch_pair = (bsend, brecv.at[cut], bss, brs)

    def share(off, incoming=False):
        origin = (cut + off) % cuts if incoming else cut
        return pltpu.make_async_remote_copy(
            src_ref=brecv.at[origin],
            dst_ref=brecv.at[origin],
            send_sem=css.at[off],
            recv_sem=crs.at[origin],
            device_id={"cuts": (cut + off) % cuts},
            device_id_type=MESH,
        )

    stem_pair = (ssend, srecv, sss, srs)
    step_pair = (tsend, trecv, tss, trs)

    pl.semaphore_wait(barrier, n - 1 + cuts - 1)
    for c in range(len(kinds)):
        for way in (UP, DOWN, ACROSS):
            send(c, me, way)
    for off in range(1, n):
        direct(branch_pair, off).start()
    loads[0].wait()
    flat = jnp.concatenate([stem[:, t * LANES : (t + 1) * LANES] for t in range(tiles)], axis=0)
    arranged = permute_bits(flat, plan).reshape(n, flat_rows // n, LANES)
    ssend[...], stem_step = encode(arranged, 1)
    tsend[:, :, :width] = jnp.broadcast_to(step.reshape(1, 1, width), (n, 1, width))
    tsend[:, :, width:] = stem_step

    for off in range(1, n):
        direct(step_pair, off).start()
    for off in range(1, n):
        direct(stem_pair, off).start()
    brecv[cut, me] = bsend[me]
    srecv[me] = ssend[me]
    trecv[me] = tsend[me]

    def relay(act, k):
        for c, kind in enumerate(kinds):
            for xo in (x, 1 - x) if kind == "A" else (x,):
                for side, way in ((-k, UP), (k, DOWN)):
                    o = (z + side) * cols + xo

                    @pl.when((z + side >= 0) & (z + side <= nz - 1))
                    def _():
                        act(c, o, way)
                        if kind == "B":
                            act(c, o, ACROSS)

    def first(c, o, way):
        if way != ACROSS:
            arrive(c, o)
        send(c, o, way)

    for c, kind in enumerate(kinds):
        if kind == "A":
            arrive(c, x_dev)
            send(c, x_dev, UP)
            send(c, x_dev, DOWN)
    relay(first, 1)
    for off in range(1, n):
        direct(branch_pair, off, True).wait_recv()
    for off in range(1, cuts):
        share(off).start()
    for k in range(2, nz):
        relay(first, k)

    def unpack(o):
        at = pl.ds(pl.multiple_of(o * rows, rows), rows)
        hi, lo = split2(decode(code[at, :], trecv[o][:, :width]))
        high[at, :] = hi
        low[at, :] = lo

    for off in range(1, n):
        direct(step_pair, off, True).wait_recv()
    for off in range(1, nz):
        unpack(((z + off) % nz) * cols + x)
    for off in range(1, cuts):
        share(off, True).wait_recv()
    plan = permute_plan([(local_bits - 1 - m, spots[m]) for m in range(local_bits)], flat_rows)
    lane_rows = one_hot(plan[0], LANES)
    first_rows[...] = one_hot(plan[1], flat_rows)
    last_rows[...] = one_hot(plan[3], flat_rows)
    last_lanes = one_hot(plan[2], LANES)
    taken = [
        lax.dot_general(
            lane_rows,
            brecv[e].reshape(n * part, quarter),
            (((0,), (0,)), ((), ())),
            preferred_element_type=jnp.float32,
        ).astype(jnp.bfloat16)
        for e in range(cuts)
    ]
    taken = jnp.concatenate(taken, axis=1)
    for off in range(1, n):
        direct(stem_pair, off, True).wait_recv()
    highs = 1 << high_bits
    got = decode(srecv[...], trecv[:, :, width:])
    lhs = jnp.concatenate([got[:, e * part : (e + 1) * part].reshape(n * part, LANES) for e in range(highs)], axis=1)
    hi, lo = split2(lhs)
    at = iota_row(n * part)
    mix = one_hot((at % part) * n + at // part, n * part)
    left_hi = dot(mix, hi).astype(jnp.bfloat16)
    left_lo = dot(mix, lo).astype(jnp.bfloat16)

    def adjoin(o):
        at = pl.ds(pl.multiple_of(o * rows, rows), rows)
        both = dot_t(jnp.concatenate([high[at, :], low[at, :]], axis=0), taken)
        adj[at, :] = both[:rows] + both[rows:]

    for off in range(nz):
        adjoin(((z + off) % nz) * cols + x)
    for off in range(nz):
        zz = (z + off) % nz
        for c, kind in enumerate(kinds):
            if kind == "B":
                arrive(c, zz * cols + (1 - x))
        unpack(zz * cols + (1 - x))
        adjoin(zz * cols + (1 - x))

    back = swap_bits(rows_times(first_rows[...], adj[...]), plan[4])
    back = lanes_times(rows_times(last_rows[...], back), last_lanes)
    for t in range(tiles):
        stem_grad[:, t * LANES : (t + 1) * LANES] = back[t * rows : (t + 1) * rows]

    branch_grad[...] = dot(left_hi, high[...]) + (dot(left_hi, low[...]) + dot(left_lo, high[...]))

    for off in range(1, cuts):
        share(off).wait_send()
    for pair in (step_pair, branch_pair, stem_pair):
        for off in range(1, n):
            direct(pair, off).wait_send()
    for c, kind in enumerate(kinds):
        for way in (UP, DOWN, ACROSS):
            sent(c, me, way)
        if kind == "A":
            sent(c, x_dev, UP)
            sent(c, x_dev, DOWN)
    for k in range(1, nz):
        relay(sent, k)


def per_device(stem_tensor, stem_cotangent, branch_tensor, bit_order):
    n, cuts = lax.axis_size("stem"), lax.axis_size("cuts")
    rows, width = stem_tensor.shape
    flat_rows = rows * width // LANES
    if n != 8 or width != n * LANES or branch_tensor.shape[0] != LANES or (rows, flat_rows) != (64, 512) or n % cuts:
        return per_device_wide(stem_tensor, stem_cotangent, branch_tensor, bit_order)
    part = branch_tensor.shape[0] // n
    vmem = pl.BlockSpec(memory_space=pltpu.VMEM)
    hbm = pl.BlockSpec(memory_space=pl.ANY)
    dma = pltpu.SemaphoreType.DMA
    return pl.pallas_call(
        functools.partial(kernel, n, cuts, KINDS),
        out_shape=(
            jax.ShapeDtypeStruct((rows, width), jnp.float32),
            jax.ShapeDtypeStruct(branch_tensor.shape, jnp.float32),
        ),
        in_specs=[pl.BlockSpec(memory_space=pltpu.SMEM), hbm, hbm, hbm],
        out_specs=(vmem, vmem),
        scratch_shapes=[
            pltpu.VMEM((rows, width), jnp.float32),
            pltpu.VMEM((rows, width), jnp.float32),
            pltpu.VMEM(branch_tensor.shape, jnp.bfloat16),
            pltpu.VMEM((n * rows, width), jnp.int16),
            pltpu.VMEM((n * rows, width), jnp.bfloat16),
            pltpu.VMEM((n * rows, width), jnp.bfloat16),
            pltpu.VMEM((n, part, width // cuts), jnp.bfloat16),
            pltpu.VMEM((cuts, n, part, width // cuts), jnp.bfloat16),
            pltpu.VMEM((n, flat_rows // n, LANES), jnp.int16),
            pltpu.VMEM((n, flat_rows // n, LANES), jnp.int16),
            pltpu.VMEM((n, 1, width + LANES), jnp.float32),
            pltpu.VMEM((n, 1, width + LANES), jnp.float32),
            dma((3,)),
            dma((len(KINDS), n, 3)),
            dma((len(KINDS), n)),
            dma((n,)),
            dma((n,)),
            dma((n,)),
            dma((n,)),
            dma((n,)),
            dma((n,)),
            dma((cuts,)),
            dma((cuts,)),
            pltpu.VMEM((flat_rows, LANES), jnp.float32),
            pltpu.VMEM((flat_rows, flat_rows), jnp.bfloat16),
            pltpu.VMEM((flat_rows, flat_rows), jnp.bfloat16),
        ],
        compiler_params=pltpu.CompilerParams(
            collective_id=0, has_side_effects=True, vmem_limit_bytes=40 * 1024 * 1024
        ),
    )(bit_order, stem_tensor, stem_cotangent, branch_tensor)


def solution(mesh):
    placed = (P(("cuts", "stem"), None), P(("cuts", "stem"), None), P("stem", None), P())
    return jax.shard_map(
        per_device,
        mesh=mesh,
        in_specs=placed,
        out_specs=(P(("cuts", "stem"), None), P(("cuts", "stem"), None)),
        check_vma=False,
    )
```
